32 devices in a mesh: cell: 4 (over x, core), gene: 8 (over z, y).
Axes of the slice: x: 2, y: 2, z: 4, core: 2. Of those that a mesh axis runs over, the one named last changes fastest.
Arguments:
- counts: int32 [4096, 8192], P('cell', 'gene'), may hold values from 0 to 4000, as said below
Outputs:
- gene_gram: float32 [8192, 8192], P('gene', 'cell')
The draws below stay inside these ranges and needn't reach their ends.
Inputs may be any that keep to these rules, and one draw needn't show every extreme that they name: `counts`: every cell and every gene has a positive count somewhere.
All inputs are finite; a program needn't handle non-finite values.
Results may differ from the reference program's by a relative error of at most 0.00054.
Values may be sent and summed in bfloat16 or wider, within the bound.
No kernel may reach another device: no remote copies, remote signals or barrier semaphores. Data moves between devices by JAX's collectives and lax.ppermute only.
A program may use at most 128 MiB of HBM per device.

```python
import jax
import jax.numpy as jnp
from jax import lax

G = 8192
CELLS = 4096


def draw_counts(key, part):
    subkeys = jax.random.split(key, 8)
    cell_index = jnp.arange(CELLS, dtype=jnp.int32)[:, None]
    gene_index = jnp.arange(G, dtype=jnp.int32)[None, :]
    cell_scale = jax.random.randint(subkeys[0], (CELLS, 1), 1, 3, dtype=jnp.int32)
    gene_scale = jax.random.randint(subkeys[1], (1, G), 1, 3, dtype=jnp.int32)
    cell_level = 1 + 3 * cell_index // CELLS
    gene_level = 1 + 3 * gene_index // G
    program = jax.random.randint(subkeys[2], (CELLS, 1), 0, 8, dtype=jnp.int32)
    module = jax.random.randint(subkeys[3], (1, G), 0, 8, dtype=jnp.int32)
    boost = 1 + (program == module).astype(jnp.int32)
    upper = cell_scale * gene_scale * cell_level * gene_level * boost
    lower = ((gene_index - cell_index) % 16 == 0).astype(jnp.int32)
    base = jax.random.randint(subkeys[4], (CELLS, G), lower, upper + 1, dtype=jnp.int32)
    spike_gene = jax.random.randint(subkeys[5], (CELLS, 1), 0, G, dtype=jnp.int32)
    spike_cell = (jax.random.randint(subkeys[6], (CELLS, 1), 0, 16, dtype=jnp.int32) == 0) | (cell_index == 0)
    spike_size = jax.random.randint(subkeys[7], (CELLS, 1), 1000, 4001, dtype=jnp.int32)
    spike_size = jnp.where(cell_index == 0, jnp.int32(4000), spike_size)
    spiked = spike_cell & (gene_index == spike_gene)
    return jnp.where(spiked, spike_size, base)


def setup_inputs(seed: int = 0) -> dict:
    streams_of = jax.random.split(jax.random.key(seed), 2)
    return {
        "counts": draw_counts(jax.random.fold_in(streams_of[1], 71), 0),
    }


def reference(counts):
    values = counts.astype(jnp.float32)
    depths = lax.optimization_barrier(jnp.sum(values, axis=1))
    gene_totals = lax.optimization_barrier(jnp.sum(values, axis=0))
    grand_total = jnp.sum(depths)
    expected = depths[:, None] * gene_totals[None, :] / grand_total
    scaled = (values - expected) / jnp.sqrt(expected + expected * expected / 100.0)
    ceiling = jnp.sqrt(jnp.float32(CELLS))
    residuals = jnp.clip(scaled, -ceiling, ceiling).astype(jnp.bfloat16)
    wide = residuals.astype(jnp.float32)
    product = lax.dot_general(wide, wide, (((0,), (0,)), ((), ())), precision=lax.Precision.HIGHEST, preferred_element_type=jnp.float32)
    return product / jnp.float32(CELLS)
```

```python
import jax
import jax.numpy as jnp
from jax import lax
from jax.sharding import PartitionSpec as P

AXES = ("cell", "gene")
UNIT = 8.0


def pairs_of(move):
    pairs = []
    for x in range(2):
        for c in range(2):
            for z in range(4):
                for y in range(2):
                    target = move(x, c, z, y)
                    if target is not None and 0 <= target[2] < 4:
                        tx, tc, tz, ty = target
                        pairs.append(((2 * x + c) * 8 + 2 * z + y, (2 * tx + tc) * 8 + 2 * tz + ty))
    return pairs


def send(value, move):
    return lax.ppermute(value, AXES, pairs_of(move))


def residuals_of(counts, depths, totals, grand, ceiling):
    expected = depths[:, None] * totals[None, :] / grand
    scaled = (counts.astype(jnp.float32) - expected) * lax.rsqrt(expected + expected * expected * 0.01)
    return jnp.clip(scaled, -ceiling, ceiling).astype(jnp.bfloat16)


def after(value, *others):
    return lax.optimization_barrier((value,) + others)[0]


def body(counts):
    cells_here, genes_here = counts.shape
    cells_all = cells_here * lax.axis_size("cell")
    half = genes_here // 2
    cell, gene = lax.axis_index("cell"), lax.axis_index("gene")
    x, c, z, y = cell // 2, cell % 2, gene // 2, gene % 2
    even = c == z % 2
    low = z < 2

    def down(distance, late):
        def move(x, c, z, y):
            source = z + distance - 1
            if c != source % 2 or source > 3 or (late and distance == 1 and x == 0 and z == 1):
                return None
            return x, c, z - 1, y
        return move

    def up(distance, late):
        def move(x, c, z, y):
            source = z - distance + 1
            if c != source % 2 or source < 0 or (late and distance == 1 and x == 1 and z == 2):
                return None
            return x, c, z + 1, y
        return move

    def last(x, c, z, y):
        if x == 0 and c == 1 and z == 1:
            return x, c, 0, y
        if x == 1 and c == 0 and z == 2:
            return x, c, 3, y
        return None

    small = counts.astype(jnp.int16)
    row_part = jnp.sum(counts, axis=1)
    totals = jnp.sum(counts, axis=0)
    small, row_part, totals = lax.optimization_barrier((small, row_part, totals))
    sibling = send(small, lambda x, c, z, y: (x, 1 - c, z, y))
    across = send(small, lambda x, c, z, y: (x, c, z, 1 - y))
    both_a = jnp.concatenate([small[:, :half], sibling[:, :half]], axis=0)
    both_b = jnp.concatenate([small[:, half:], sibling[:, half:]], axis=0)
    d1a, u1a = send(both_a, down(1, False)), send(both_a, up(1, False))
    d1b, u1b = send(both_b, down(1, True)), send(both_b, up(1, True))

    row_part, totals, both_a, both_b = lax.optimization_barrier((row_part, totals, both_a, both_b))
    totals = totals + send(totals, lambda x, c, z, y: (x, 1 - c, z, y))
    totals = totals + send(totals, lambda x, c, z, y: (1 - x, c, z, y))
    got = send(jnp.concatenate([totals, row_part]), lambda x, c, z, y: (x, c, z, 1 - y))
    totals = jnp.concatenate([totals, got[:genes_here]])
    depths = row_part + got[genes_here:]
    for bit in (1, 2):
        got = send(jnp.concatenate([totals, depths]), lambda x, c, z, y: (x, c, z ^ bit, y))
        depths = depths + got[totals.size :]
        totals = jnp.concatenate([totals, got[: totals.size]])
    depths = jnp.stack([depths, send(depths, lambda x, c, z, y: (x, 1 - c, z, y))])
    depths = depths.reshape(-1).astype(jnp.float32)
    totals = totals.astype(jnp.float32).reshape(4, 2, genes_here)
    grand = jnp.sum(totals)
    ceiling = jnp.sqrt(jnp.float32(cells_all))

    def totals_of(block):
        index = block ^ z
        out = totals[0, 0]
        for i in range(1, 4):
            out = jnp.where(index == i, totals[i, 0], out)
        return out

    def convert(values, gene_totals):
        return residuals_of(values, depths, gene_totals, grand, ceiling)

    def gram(left, right):
        product = lax.dot_general(
            left, right, (((0,), (0,)), ((), ())), preferred_element_type=jnp.float32
        )
        return (product * (UNIT / cells_all)).astype(jnp.float16)

    def cross(value, remote):
        return send(value, lambda x, c, z, y: (1 - x, c, z, y) if remote(x, c, z) else None)

    def is_even(c, z):
        return c == z % 2

    rows_own = convert(jnp.concatenate([both_a, both_b], axis=1), totals[0, 0])
    p0_own = gram(rows_own, rows_own)
    remote0 = lambda x, c, z: is_even(c, z) and x != z // 2
    x0_own = cross(p0_own, remote0)

    d2a, u2a = send(d1a, down(2, False)), send(u1a, up(2, False))
    d2b, u2b = send(d1b, down(2, False)), send(u1b, up(2, False))

    across_sibling = send(across, lambda x, c, z, y: (x, 1 - c, z, y))
    rows_other = convert(jnp.concatenate([across, across_sibling], axis=0), totals[0, 1])
    rows = jnp.concatenate([rows_own, rows_other], axis=1)
    p0_other = gram(rows_other, rows_own)
    x0_other = cross(p0_other, remote0)

    take_down = jnp.where(z == 0, True, jnp.where(z == 3, False, x == 0))
    take_down = jnp.where((z == 2), x == 0, take_down)
    first_a = jnp.where(take_down, d1a, u1a)
    first_b = jnp.where(take_down, d1b, u1b)
    p1 = gram(
        rows,
        convert(
            jnp.concatenate([first_a, first_b], axis=1),
            totals_of(jnp.where(take_down, z + 1, z - 1)),
        ),
    )
    def remote1(x, c, z):
        return not is_even(c, z) and (x, z) not in ((0, 0), (1, 3))
    x1 = cross(p1, remote1)

    d3a, u3a = send(d2a, down(3, False)), send(u2a, up(3, False))

    far_totals = totals_of(jnp.where(low, z + 2, z - 2))
    p2a = gram(rows, convert(jnp.where(low, d2a, u2a), far_totals[:half]))
    remote2 = lambda x, c, z: is_even(c, z) and x == z // 2
    x2a = cross(p2a, remote2)
    d3b, u3b = send(d2b, down(3, False)), send(u2b, up(3, False))
    p2b = gram(rows, convert(jnp.where(low, d2b, u2b), far_totals[half:]))
    x2b = cross(p2b, remote2)
    late = send(after(both_b, d3b, u3b), last)

    end = (z == 0) | (z == 3)
    far_x = (x == 0) == (z == 0)
    end_totals = totals_of(3 - z)
    near_totals = totals_of(jnp.where(take_down, z - 1, z + 1))
    p3a = gram(rows, convert(jnp.where(low, d3a, u3a), end_totals[:half]))
    remote3 = lambda x, c, z: (x, c, z) in ((0, 1, 0), (1, 0, 3))
    x3a = cross(p3a, remote3)
    middle_a = jnp.where(take_down, u1a, d1a)
    end_a = jnp.where(far_x, jnp.where(low, d3b, u3b), jnp.where(low, d3a, u3a))
    p4 = gram(
        rows,
        convert(
            jnp.where(end, end_a, middle_a),
            jnp.where(end, jnp.where(far_x, end_totals[half:], end_totals[:half]), near_totals[:half]),
        ),
    )
    x3b = cross(p4, remote3)
    middle_b = jnp.where(take_down, u1b, d1b)
    end_b = jnp.where(far_x, late, jnp.where(low, d3b, u3b))
    late_totals = totals_of(jnp.where(z == 0, 1, 2))
    p5 = gram(
        rows,
        convert(
            jnp.where(end, end_b, middle_b),
            jnp.where(end, jnp.where(far_x, late_totals[half:], end_totals[half:]), near_totals[half:]),
        ),
    )

    def swap(value):
        return send(value, lambda x, c, z, y: (x, c, z, 1 - y))

    wide = lambda value: value.astype(jnp.float32)

    keeps_own = x == z // 2
    p2 = jnp.concatenate([p2a, p2b], axis=1)
    x2 = jnp.concatenate([x2a, x2b], axis=1)
    even_own = jnp.where(keeps_own, wide(p0_own) + wide(x0_own), wide(p2[:genes_here]) + wide(x2[:genes_here]))
    even_other = jnp.where(
        keeps_own, wide(p0_other) + wide(x0_other), wide(p2[genes_here:]) + wide(x2[genes_here:])
    ).astype(jnp.float16)
    even_got = swap(even_other)

    far_keep = end & jnp.logical_not(far_x)
    odd_a = wide(jnp.where(end & far_x, p1[:, :half], p4)) + wide(jnp.where(far_keep, x3a, x1[:, :half]))
    odd_b = wide(p5) + wide(jnp.where(far_keep, x3b, x1[:, half:]))
    got_a = swap(odd_a[genes_here:].astype(jnp.float16))
    got_b = swap(odd_b[genes_here:].astype(jnp.float16))

    out = jnp.concatenate([even_own, wide(even_got)], axis=1)
    first, second = y * genes_here, (1 - y) * genes_here
    out = jnp.where(y == 0, out, jnp.concatenate([wide(even_got), even_own], axis=1)) * (1.0 / UNIT)
    for value, got, offset in ((odd_a, got_a, 0), (odd_b, got_b, half)):
        for piece, start in ((value[:genes_here], first + offset), (wide(got), second + offset)):
            old = lax.dynamic_slice(out, (0, start), (genes_here, half))
            out = lax.dynamic_update_slice(out, jnp.where(even, old, piece * (1.0 / UNIT)), (0, start))
    return out


def body_any(counts):
    cells_all = counts.shape[0] * lax.axis_size("cell")
    values = counts.astype(jnp.float32)
    row_part = jnp.sum(values, axis=1)
    column_part = jnp.sum(values, axis=0)
    depths = lax.psum(row_part, "gene")
    gene_totals, grand_total = lax.psum((column_part, jnp.sum(depths)), "cell")
    expected = depths[:, None] * gene_totals[None, :] / grand_total
    scaled = (values - expected) / jnp.sqrt(expected + expected * expected / 100.0)
    ceiling = jnp.sqrt(jnp.float32(cells_all))
    residuals = jnp.clip(scaled, -ceiling, ceiling).astype(jnp.bfloat16)
    gathered = lax.all_gather(residuals, "gene", axis=1, tiled=True)
    owned_block = lax.psum_scatter(
        lax.dot_general(
            gathered, residuals, (((0,), (0,)), ((), ())), preferred_element_type=jnp.float32
        ),
        "cell",
        scatter_dimension=0,
        tiled=True,
    ).T
    return owned_block / jnp.float32(cells_all)


def solution(mesh):
    fits = (mesh.shape["cell"], mesh.shape["gene"]) == (4, 8)
    return jax.shard_map(
        body if fits else body_any,
        mesh=mesh,
        in_specs=(P("cell", "gene"),),
        out_specs=P("gene", "cell"),
        check_vma=False,
    )
```

```python
import math

import jax
import jax.numpy as jnp
import numpy as np
from jax import lax
from jax.experimental import pallas as pl
from jax.experimental.pallas import tpu as pltpu
from jax.sharding import PartitionSpec as P

AXES = ("cell", "gene")
UNIT = 8.0


def pairs_of(move):
    pairs = []
    for x in range(2):
        for c in range(2):
            for z in range(4):
                for y in range(2):
                    target = move(x, c, z, y)
                    if target is not None and 0 <= target[2] < 4:
                        tx, tc, tz, ty = target
                        pairs.append(((2 * x + c) * 8 + 2 * z + y, (2 * tx + tc) * 8 + 2 * tz + ty))
    return pairs


def send(value, move):
    return lax.ppermute(value, AXES, pairs_of(move))


def after(value, *others):
    return lax.optimization_barrier((value,) + others)[0]


VMEM = 48 * 2**20
SLOTS = 6


def residuals_of(near, far, depths, shares, part, parts, ceiling):
    cells, genes = near.shape
    width = genes // parts
    block = 512
    steps = cells // block
    lanes, group = 128, 32

    def kernel(part_ref, depth_ref, share_ref, near_ref, far_ref, out_ref):
        i = pl.program_id(0)
        depth = jnp.transpose(jnp.broadcast_to(depth_ref[...], (lanes, block)))

        def write(counts_ref):
            for r in range(0, block, group):
                for k in range(0, width, lanes):
                    expected = depth[r : r + group] * share_ref[:, k : k + lanes]
                    scale = lax.rsqrt(expected + expected * expected * 0.01)
                    values = counts_ref[r : r + group, k : k + lanes].astype(jnp.float32)
                    scaled = jnp.clip((values - expected) * scale, -ceiling, ceiling)
                    out_ref[r : r + group, k : k + lanes] = scaled.astype(jnp.bfloat16)

        @pl.when(i < steps)
        def _():
            write(near_ref)

        @pl.when(i >= steps)
        def _():
            write(far_ref)

    return pl.pallas_call(
        kernel,
        grid_spec=pltpu.PrefetchScalarGridSpec(
            num_scalar_prefetch=1,
            grid=(2 * steps,),
            in_specs=[
                pl.BlockSpec((1, block), lambda i, s: (0, i)),
                pl.BlockSpec((1, width), lambda i, s: (0, s[0])),
                pl.BlockSpec((block, width), lambda i, s: (jnp.minimum(i, steps - 1), s[0])),
                pl.BlockSpec((block, width), lambda i, s: (jnp.maximum(i - steps, 0), s[0])),
            ],
            out_specs=pl.BlockSpec((block, width), lambda i, s: (i, 0)),
        ),
        out_shape=jax.ShapeDtypeStruct((2 * cells, width), jnp.bfloat16),
        compiler_params=pltpu.CompilerParams(vmem_limit_bytes=VMEM),
        cost_estimate=pl.CostEstimate(
            flops=20 * cells * width, bytes_accessed=12 * cells * width, transcendentals=2 * cells * width
        ),
    )(jnp.reshape(part, (1,)).astype(jnp.int32), depths.reshape(1, -1), shares.reshape(1, -1), near, far)


def products_of(plan, slot, lefts, turned, rights):
    rows, width = rights[0].shape
    blocks, upper = 4, rows // 2
    n_left = len(lefts)

    def kernel(s, *refs):
        left_refs, right_refs = refs[:n_left], refs[n_left : n_left + len(rights)]
        out_ref, left_buf, right_buf, left_sem, right_sem = refs[n_left + len(rights) :]
        i = pl.program_id(0)

        def left_at(block):
            return s[slot * 2 * blocks + 2 * block]

        def right_at(block):
            return s[slot * 2 * blocks + 2 * block + 1]

        def left_copies(n, to):
            for part in range(2):
                place = 1 - part if turned[n] else part
                yield pltpu.make_async_copy(
                    left_refs[n].at[pl.ds(part * upper, upper)],
                    left_buf.at[to, pl.ds(place * upper, upper)],
                    left_sem.at[to, part],
                )

        def fetch(block, to):
            for n in range(n_left):
                @pl.when(left_at(block) == n)
                def _(n=n):
                    for copy in left_copies(n, to):
                        copy.start()

        def arrive(block, to):
            for n in range(n_left):
                @pl.when(left_at(block) == n)
                def _(n=n):
                    for copy in left_copies(n, to):
                        copy.wait()

        @pl.when(i == 0)
        def _():
            fetch(0, 0)

        @pl.when((i == 0) | (right_at(i) != right_at(jnp.maximum(i - 1, 0))))
        def _():
            for n, ref in enumerate(right_refs):
                @pl.when(right_at(i) == n)
                def _(ref=ref):
                    copy = pltpu.make_async_copy(ref, right_buf, right_sem)
                    copy.start()
                    copy.wait()

        for to in range(2):
            @pl.when(lax.rem(i, 2) == to)
            def _(to=to):
                arrive(i, to)

                @pl.when(i + 1 < blocks)
                def _():
                    fetch(i + 1, 1 - to)

                out_ref[...] = lax.dot_general(
                    left_buf[to], right_buf[...], (((0,), (0,)), ((), ())), preferred_element_type=jnp.float32
                )

    return pl.pallas_call(
        kernel,
        grid_spec=pltpu.PrefetchScalarGridSpec(
            num_scalar_prefetch=1,
            grid=(blocks,),
            in_specs=[pl.BlockSpec(memory_space=pl.ANY)] * (n_left + len(rights)),
            out_specs=pl.BlockSpec((width, width), lambda i, s: (i, 0)),
            scratch_shapes=[
                pltpu.VMEM((2, rows, width), jnp.bfloat16),
                pltpu.VMEM((rows, width), jnp.bfloat16),
                pltpu.SemaphoreType.DMA((2, 2)),
                pltpu.SemaphoreType.DMA,
            ],
        ),
        out_shape=jax.ShapeDtypeStruct((blocks * width, width), jnp.float32),
        compiler_params=pltpu.CompilerParams(vmem_limit_bytes=VMEM),
        cost_estimate=pl.CostEstimate(
            flops=8 * rows * blocks * width * width,
            bytes_accessed=2 * (blocks + 1) * rows * width + 4 * blocks * width * width,
            transcendentals=0,
        ),
    )(plan, *lefts, *rights)


def is_even(c, z):
    return c == z % 2


def is_near(x, z):
    return x == z // 2


def is_end(z):
    return z in (0, 3)


def job(x, c, z, slot):
    near, first = is_near(x, z), 1 if z == 0 or (z != 3 and x == 0) else -1
    far = 2 if z < 2 else -2
    if is_even(c, z):
        if slot == 0:
            return "own rows", not near
        if not near:
            return [None, ("other rows", True), None, ((far, 0), False), ((far, 1), False), None][slot]
        if is_end(z):
            return [None, ((far, 0), True), ((far, 1), True), ("other rows", False), None, None][slot]
        return [None, ("other rows", False), ((far, 0), True), ((far, 1), True), None, None][slot]
    if not is_end(z):
        return [None, ((first, 0), True), ((first, 1), True), ((-first, 0), False), ((-first, 1), False), None][slot]
    far = 3 if z == 0 else -3
    if near:
        return [None, ((first, 0), False), None, ((far, 0), True), ((far, 1), True), ((first, 1), False)][slot]
    return [None, ((first, 0), True), ((first, 1), True), None, ((far, 0), False), ((far, 1), False)][slot]


def remote(slot):
    def devices(x, c, z):
        work = job(x, c, z, slot)
        return work is not None and work[1]
    return devices


def rights_of(slot):
    names, table = [("own", 0), ("own", 1)] if slot < 4 else [], np.zeros((2, 2, 4, 4, 2), np.int32)
    for x in range(2):
        for c in range(2):
            for z in range(4):
                work = job(x, c, z, slot)
                if work is None:
                    continue
                if work[0] in ("own rows", "other rows"):
                    rows = (0, 1) if work[0] == "own rows" else (2, 3)
                    pairs = [(row, ("own", half)) for half in range(2) for row in rows]
                else:
                    name = ("late", 0) if slot == 5 and abs(work[0][0]) == 1 else work[0]
                    pairs = [(row, name) for row in range(4)]
                for i, (row, name) in enumerate(pairs):
                    if name not in names:
                        names.append(name)
                    table[x, c, z, i] = row, names.index(name)
    return names, table


def body(counts):
    cells_here, genes_here = counts.shape
    cells_all = cells_here * lax.axis_size("cell")
    half = genes_here // 2
    cell, gene = lax.axis_index("cell"), lax.axis_index("gene")
    x, c, z, y = cell // 2, cell % 2, gene // 2, gene % 2
    even = c == z % 2
    low = z < 2
    end = (z == 0) | (z == 3)
    odd_end = end & jnp.logical_not(even)
    near_x = (x == 0) == low

    def is_odd_end(c, z):
        return not is_even(c, z) and is_end(z)

    def down(distance):
        def move(x, c, z, y):
            source = z + distance - 1
            if c != source % 2 or source > 3 or (distance == 1 and x == 0 and z == 1):
                return None
            return x, c, z - 1, y
        return move

    def up(distance):
        def move(x, c, z, y):
            source = z - distance + 1
            if c != source % 2 or source < 0 or (distance == 1 and x == 1 and z == 2):
                return None
            return x, c, z + 1, y
        return move

    def last(x, c, z, y):
        if x == 0 and c == 1 and z == 1:
            return x, c, 0, y
        if x == 1 and c == 0 and z == 2:
            return x, c, 3, y
        return None

    def down_all(x, c, z, y):
        return (x, c, z - 1, y) if c == z % 2 else None

    def up_all(x, c, z, y):
        return (x, c, z + 1, y) if c == z % 2 else None

    def swap_core(value):
        return send(value, lambda x, c, z, y: (x, 1 - c, z, y))

    def swap_y(value, devices=lambda x, c, z: True):
        return send(value, lambda x, c, z, y: (x, c, z, 1 - y) if devices(x, c, z) else None)

    def cross(value, devices):
        return send(value, lambda x, c, z, y: (1 - x, c, z, y) if devices(x, c, z) else None)

    sibling = swap_core(counts)
    row_part = jnp.sum(counts, axis=1)
    totals = jnp.sum(counts, axis=0)
    both = swap_core(jnp.concatenate([totals, row_part]))
    beside = [
        send(totals, lambda x, c, z, y: (1 - x, c, z, y)),
        send(totals, lambda x, c, z, y: (1 - x, 1 - c, z, y)),
    ]
    totals = totals + both[:genes_here] + beside[0] + beside[1]
    row_part = jnp.concatenate([row_part, both[genes_here:]])
    got = swap_y(jnp.concatenate([totals, row_part]))
    message = jnp.concatenate([totals, got[:genes_here], row_part + got[genes_here:]])
    messages = jnp.stack(
        [message]
        + [send(message, lambda x, c, z, y, bits=bits: (x, c, z ^ bits, y)) for bits in (1, 2, 3)]
    )
    depths = jnp.sum(messages[:, 2 * genes_here :], axis=0).astype(jnp.float32)
    grand = jnp.sum(messages[:, : 2 * genes_here].astype(jnp.float32))
    ceiling = math.sqrt(cells_all)
    shares = totals.astype(jnp.float32) / grand

    own_a = residuals_of(counts, sibling, depths, shares, c, 2, ceiling)
    d1a, u1a = send(own_a, down_all), send(own_a, up_all)
    own_b = residuals_of(counts, sibling, depths, shares, 1 - c, 2, ceiling)
    d1b, u1b = send(own_b, down(1)), send(own_b, up(1))
    across = swap_y(after(own_a, own_b))

    jobs = [rights_of(slot) for slot in range(SLOTS)]
    tables = np.stack([table for _, table in jobs], axis=3)
    tables[:, 1, :, :, :, 0] ^= 1
    plan = jnp.asarray(tables.reshape(16, -1))[(2 * x + c) * 4 + z]
    out = jnp.full((genes_here, 2 * genes_here), grand * 0.0)
    scale = UNIT / cells_all
    held = {("own", 0): own_a, ("own", 1): own_b, (1, 0): d1a, (-1, 0): u1a, (1, 1): d1b, (-1, 1): u1b}
    products, narrow_products, received = [], [], []

    def work(slot, lefts, plan):
        product = products_of(plan, slot, lefts, [False, False, False, True], [held[n] for n in jobs[slot][0]])
        products.append(product)
        if slot < SLOTS - 1:
            narrow_products.append((product * scale).astype(jnp.float16))
            received.append(cross(narrow_products[-1], remote(slot)))

    work(0, [own_a, own_b], plan)
    d2a, u2a = send(d1a, down(2)), send(u1a, up(2))
    d1b, u1b, out, _ = lax.optimization_barrier((d1b, u1b, out, narrow_products[0]))
    held[1, 1], held[-1, 1], held[2, 0], held[-2, 0] = d1b, u1b, d2a, u2a
    d2b, u2b = send(d1b, down(2)), send(u1b, up(2))
    held[2, 1], held[-2, 1] = d2b, u2b
    lefts = [own_a, own_b, across, swap_core(across)]
    plan, out = lax.optimization_barrier((plan, out))
    work(1, lefts, plan)
    d2a, u2a, _ = lax.optimization_barrier((d2a, u2a, narrow_products[1]))
    d3a, u3a = send(d2a, down(3)), send(u2a, up(3))
    d3b, u3b = send(d2b, down(3)), send(u2b, up(3))
    work(2, lefts, after(plan, narrow_products[1], received[0]))
    held[3, 0], held[-3, 0], held[3, 1], held[-3, 1] = d3a, u3a, d3b, u3b
    work(3, lefts, after(plan, narrow_products[2]))
    held["late", 0] = send(after(own_b, d3b, u3b), last)
    work(4, lefts, after(plan, narrow_products[3], received[1]))

    wide = lambda value: value.astype(jnp.float32)
    low_rows, high_rows = slice(0, genes_here), slice(genes_here, None)

    def own_rows(half):
        return low_rows

    def mix(choices):
        value = choices[-1][1]
        for condition, other in reversed(choices[:-1]):
            value = jnp.where(condition, other, value)
        return value

    near_even, far_even = even & near_x, even & jnp.logical_not(near_x)
    near_end = odd_end & near_x
    far_end = odd_end & jnp.logical_not(near_x)

    def sums(other, half):
        rows = high_rows if other else low_rows
        stacked = high_rows if half else low_rows
        p, r = products, received
        own_block = mix([(end, p[3][stacked]), (None, p[1][stacked])]) if other else p[0][stacked]
        own_received = r[1][stacked] if other else r[0][stacked]
        if half == 0:
            mine = [(near_even, own_block), (near_end, p[1][rows]), (far_end, p[4][rows]), (None, p[3][rows])]
            far_received = mix([(end, r[1][rows]), (None, r[2][rows])])
            theirs = [(near_even, own_received), (far_even, far_received), (far_end, r[3][rows]), (None, r[1][rows])]
        else:
            mine = [(near_even, own_block), (odd_end, p[5][rows]), (None, p[4][rows])]
            far_received = mix([(end, r[2][rows]), (None, r[3][rows])])
            theirs = [(near_even, own_received), (far_even, far_received), (far_end, r[4][rows]), (None, r[2][rows])]
        return mix(mine) * scale + wide(mix(theirs))

    narrow = lambda value: value.astype(jnp.float16)

    def is_far_end(x, c, z):
        return is_odd_end(c, z) and not is_near(x, z)

    other_a = sums(True, 0)
    got_first = swap_y(narrow(other_a), lambda x, c, z: not is_far_end(x, c, z))
    work(5, lefts, after(plan, narrow_products[4], received[2], narrow(other_a)))
    other_b = sums(True, 1)
    middle = jnp.where(odd_end, other_a, other_b)
    got_middle = swap_y(narrow(middle), lambda x, c, z: not is_odd_end(c, z) or is_far_end(x, c, z))
    got_last = swap_y(narrow(other_b), lambda x, c, z: is_odd_end(c, z))
    got_a = jnp.where(far_end, got_middle, got_first)
    got_b = jnp.where(odd_end, got_last, got_middle)

    begin, begin_other = y * genes_here, (1 - y) * genes_here
    for half_of, got in ((0, got_a), (1, got_b)):
        place = (half_of ^ c) * half
        out = lax.dynamic_update_slice(out, sums(False, half_of) * (1.0 / UNIT), (0, begin + place))
        out = lax.dynamic_update_slice(out, wide(got) * (1.0 / UNIT), (0, begin_other + place))
    return out


def body_any(counts):
    cells_all = counts.shape[0] * lax.axis_size("cell")
    values = counts.astype(jnp.float32)
    row_part = jnp.sum(values, axis=1)
    column_part = jnp.sum(values, axis=0)
    depths = lax.psum(row_part, "gene")
    gene_totals, grand_total = lax.psum((column_part, jnp.sum(depths)), "cell")
    expected = depths[:, None] * gene_totals[None, :] / grand_total
    scaled = (values - expected) / jnp.sqrt(expected + expected * expected / 100.0)
    ceiling = jnp.sqrt(jnp.float32(cells_all))
    residuals = jnp.clip(scaled, -ceiling, ceiling).astype(jnp.bfloat16)
    gathered = lax.all_gather(residuals, "gene", axis=1, tiled=True)
    owned_block = lax.psum_scatter(
        lax.dot_general(
            gathered, residuals, (((0,), (0,)), ((), ())), preferred_element_type=jnp.float32
        ),
        "cell",
        scatter_dimension=0,
        tiled=True,
    ).T
    return owned_block / jnp.float32(cells_all)


def solution(mesh):
    fits = (mesh.shape["cell"], mesh.shape["gene"]) == (4, 8)
    return jax.shard_map(
        body if fits else body_any,
        mesh=mesh,
        in_specs=(P("cell", "gene"),),
        out_specs=P("gene", "cell"),
        check_vma=False,
    )
```

```python
import math

import jax
import jax.numpy as jnp
import numpy as np
from jax import lax
from jax.experimental import pallas as pl
from jax.experimental.pallas import tpu as pltpu
from jax.sharding import PartitionSpec as P

AXES = ("cell", "gene")
UNIT = 8.0


def pairs_of(move):
    pairs = []
    for x in range(2):
        for c in range(2):
            for z in range(4):
                for y in range(2):
                    target = move(x, c, z, y)
                    if target is not None and 0 <= target[2] < 4:
                        tx, tc, tz, ty = target
                        pairs.append(((2 * x + c) * 8 + 2 * z + y, (2 * tx + tc) * 8 + 2 * tz + ty))
    return pairs


def send(value, move):
    return lax.ppermute(value, AXES, pairs_of(move))


def after(value, *others):
    return lax.optimization_barrier((value,) + others)[0]


VMEM = 48 * 2**20
SLOTS = 6
LIGHT = pl.CostEstimate(flops=0, bytes_accessed=0, transcendentals=0)


def residuals_of(near, far, depths, shares, part, parts, ceiling):
    cells, genes = near.shape
    width = genes // parts
    block = 512
    steps = cells // block
    lanes, group = 128, 32

    def kernel(part_ref, depth_ref, share_ref, near_ref, far_ref, out_ref):
        i = pl.program_id(0)
        depth = jnp.transpose(jnp.broadcast_to(depth_ref[...], (lanes, block)))

        def write(counts_ref):
            for r in range(0, block, group):
                for k in range(0, width, lanes):
                    expected = depth[r : r + group] * share_ref[:, k : k + lanes]
                    scale = lax.rsqrt(expected + expected * expected * 0.01)
                    values = counts_ref[r : r + group, k : k + lanes].astype(jnp.float32)
                    scaled = jnp.clip((values - expected) * scale, -ceiling, ceiling)
                    out_ref[r : r + group, k : k + lanes] = scaled.astype(jnp.bfloat16)

        @pl.when(i < steps)
        def _():
            write(near_ref)

        @pl.when(i >= steps)
        def _():
            write(far_ref)

    return pl.pallas_call(
        kernel,
        grid_spec=pltpu.PrefetchScalarGridSpec(
            num_scalar_prefetch=1,
            grid=(2 * steps,),
            in_specs=[
                pl.BlockSpec((1, block), lambda i, s: (0, i)),
                pl.BlockSpec((1, width), lambda i, s: (0, s[0])),
                pl.BlockSpec((block, width), lambda i, s: (jnp.minimum(i, steps - 1), s[0])),
                pl.BlockSpec((block, width), lambda i, s: (jnp.maximum(i - steps, 0), s[0])),
            ],
            out_specs=pl.BlockSpec((block, width), lambda i, s: (i, 0)),
        ),
        out_shape=jax.ShapeDtypeStruct((2 * cells, width), jnp.bfloat16),
        compiler_params=pltpu.CompilerParams(vmem_limit_bytes=VMEM),
        cost_estimate=pl.CostEstimate(
            flops=20 * cells * width, bytes_accessed=12 * cells * width, transcendentals=2 * cells * width
        ),
    )(jnp.reshape(part, (1,)).astype(jnp.int32), depths.reshape(1, -1), shares.reshape(1, -1), near, far)


def products_of(plan, slot, lefts, turned, rights, first=0, blocks=4):
    rows, width = rights[0].shape
    upper = rows // 2
    base = (slot * 4 + first) * 2
    n_left = len(lefts)

    def kernel(s, *refs):
        left_refs, right_refs = refs[:n_left], refs[n_left : n_left + len(rights)]
        out_ref, left_buf, right_buf, left_sem, right_sem = refs[n_left + len(rights) :]
        i = pl.program_id(0)

        def left_at(block):
            return s[base + 2 * block]

        def right_at(block):
            return s[base + 2 * block + 1]

        def left_copies(n, to):
            for part in range(2):
                place = 1 - part if turned[n] else part
                yield pltpu.make_async_copy(
                    left_refs[n].at[pl.ds(part * upper, upper)],
                    left_buf.at[to, pl.ds(place * upper, upper)],
                    left_sem.at[to, part],
                )

        def fetch(block, to):
            for n in range(n_left):
                @pl.when(left_at(block) == n)
                def _(n=n):
                    for copy in left_copies(n, to):
                        copy.start()

        def arrive(block, to):
            for n in range(n_left):
                @pl.when(left_at(block) == n)
                def _(n=n):
                    for copy in left_copies(n, to):
                        copy.wait()

        @pl.when(i == 0)
        def _():
            fetch(0, 0)

        @pl.when((i == 0) | (right_at(i) != right_at(jnp.maximum(i - 1, 0))))
        def _():
            for n, ref in enumerate(right_refs):
                @pl.when(right_at(i) == n)
                def _(ref=ref):
                    copy = pltpu.make_async_copy(ref, right_buf, right_sem)
                    copy.start()
                    copy.wait()

        for to in range(2):
            @pl.when(lax.rem(i, 2) == to)
            def _(to=to):
                arrive(i, to)

                @pl.when(i + 1 < blocks)
                def _():
                    fetch(i + 1, 1 - to)

                out_ref[...] = lax.dot_general(
                    left_buf[to], right_buf[...], (((0,), (0,)), ((), ())), preferred_element_type=jnp.float32
                )

    return pl.pallas_call(
        kernel,
        grid_spec=pltpu.PrefetchScalarGridSpec(
            num_scalar_prefetch=1,
            grid=(blocks,),
            in_specs=[pl.BlockSpec(memory_space=pl.ANY)] * (n_left + len(rights)),
            out_specs=pl.BlockSpec((width, width), lambda i, s: (i, 0)),
            scratch_shapes=[
                pltpu.VMEM((2, rows, width), jnp.bfloat16),
                pltpu.VMEM((rows, width), jnp.bfloat16),
                pltpu.SemaphoreType.DMA((2, 2)),
                pltpu.SemaphoreType.DMA,
            ],
        ),
        out_shape=jax.ShapeDtypeStruct((blocks * width, width), jnp.float32),
        compiler_params=pltpu.CompilerParams(vmem_limit_bytes=VMEM),
        cost_estimate=pl.CostEstimate(
            flops=8 * rows * blocks * width * width,
            bytes_accessed=2 * (blocks + 1) * rows * width + 4 * blocks * width * width,
            transcendentals=0,
        ),
    )(plan, *lefts, *rights)


def is_even(c, z):
    return c == z % 2


def is_near(x, z):
    return x == z // 2


def is_end(z):
    return z in (0, 3)


def job(x, c, z, slot):
    near, first = is_near(x, z), 1 if z == 0 or (z != 3 and x == 0) else -1
    far = 2 if z < 2 else -2
    if is_even(c, z):
        if slot == 0:
            return "own rows", not near
        if not near:
            return [None, ("other rows", True), None, ((far, 0), False), ((far, 1), False), None][slot]
        return [None, ("other rows", False), ((far, 0), True), ((far, 1), True), None, None][slot]
    if not is_end(z):
        return [None, ((first, 0), True), ((first, 1), True), ((-first, 0), False), ((-first, 1), False), None][slot]
    far = 3 if z == 0 else -3
    if near:
        return [None, ((first, 0), False), None, ((far, 0), True), ((far, 1), True), ((first, 1), False)][slot]
    return [None, ((first, 0), True), ((first, 1), True), None, ((far, 0), False), ((far, 1), False)][slot]


def remote(slot):
    def devices(x, c, z):
        work = job(x, c, z, slot)
        return work is not None and work[1]
    return devices


def rights_of(slot):
    names, table = [("own", 0), ("own", 1)] if slot < 2 else [], np.zeros((2, 2, 4, 4, 2), np.int32)
    for x in range(2):
        for c in range(2):
            for z in range(4):
                work = job(x, c, z, slot)
                if work is None:
                    continue
                if work[0] in ("own rows", "other rows"):
                    rows = (0, 1) if work[0] == "own rows" else (2, 3)
                    pairs = [(row, ("own", half)) for half in range(2) for row in rows]
                else:
                    name = ("late", 0) if slot == 5 and abs(work[0][0]) == 1 else work[0]
                    pairs = [(row, name) for row in range(4)]
                for i, (row, name) in enumerate(pairs):
                    if name not in names:
                        names.append(name)
                    table[x, c, z, i] = row, names.index(name)
    return names, table


def body(counts):
    cells_here, genes_here = counts.shape
    cells_all = cells_here * lax.axis_size("cell")
    half = genes_here // 2
    cell, gene = lax.axis_index("cell"), lax.axis_index("gene")
    x, c, z, y = cell // 2, cell % 2, gene // 2, gene % 2
    even = c == z % 2
    low = z < 2
    end = (z == 0) | (z == 3)
    odd_end = end & jnp.logical_not(even)
    near_x = (x == 0) == low

    def is_odd_end(c, z):
        return not is_even(c, z) and is_end(z)

    def down(distance):
        def move(x, c, z, y):
            source = z + distance - 1
            if c != source % 2 or source > 3 or (distance == 1 and x == 0 and z == 1):
                return None
            return x, c, z - 1, y
        return move

    def up(distance):
        def move(x, c, z, y):
            source = z - distance + 1
            if c != source % 2 or source < 0 or (distance == 1 and x == 1 and z == 2):
                return None
            return x, c, z + 1, y
        return move

    def last(x, c, z, y):
        if x == 0 and c == 1 and z == 1:
            return x, c, 0, y
        if x == 1 and c == 0 and z == 2:
            return x, c, 3, y
        return None

    def down_all(x, c, z, y):
        return (x, c, z - 1, y) if c == z % 2 else None

    def up_all(x, c, z, y):
        return (x, c, z + 1, y) if c == z % 2 else None

    def swap_core(value):
        return send(value, lambda x, c, z, y: (x, 1 - c, z, y))

    def swap_y(value, devices=lambda x, c, z: True):
        return send(value, lambda x, c, z, y: (x, c, z, 1 - y) if devices(x, c, z) else None)

    def cross(value, devices):
        return send(value, lambda x, c, z, y: (1 - x, c, z, y) if devices(x, c, z) else None)

    sibling = swap_core(counts)
    row_part = jnp.sum(counts, axis=1)
    totals = jnp.sum(counts, axis=0)
    both = swap_core(jnp.concatenate([totals, row_part]))
    beside = [
        send(totals, lambda x, c, z, y: (1 - x, c, z, y)),
        send(totals, lambda x, c, z, y: (1 - x, 1 - c, z, y)),
    ]
    totals = totals + both[:genes_here] + beside[0] + beside[1]
    row_part = jnp.concatenate([row_part, both[genes_here:]])
    got = swap_y(jnp.concatenate([totals, row_part]))
    message = jnp.concatenate([totals, got[:genes_here], row_part + got[genes_here:]])
    messages = jnp.stack(
        [message]
        + [send(message, lambda x, c, z, y, bits=bits: (x, c, z ^ bits, y)) for bits in (1, 2, 3)]
    )
    depths = jnp.sum(messages[:, 2 * genes_here :], axis=0).astype(jnp.float32)
    grand = jnp.sum(messages[:, : 2 * genes_here].astype(jnp.float32))
    ceiling = math.sqrt(cells_all)
    shares = totals.astype(jnp.float32) / grand

    own_a = residuals_of(counts, sibling, depths, shares, c, 2, ceiling)
    d1a, u1a = send(own_a, down_all), send(own_a, up_all)
    own_b = residuals_of(counts, sibling, depths, shares, 1 - c, 2, ceiling)
    d1b, u1b = send(own_b, down(1)), send(own_b, up(1))
    across = swap_y(after(own_a, own_b))

    jobs = [rights_of(slot) for slot in range(SLOTS)]
    tables = np.stack([table for _, table in jobs], axis=3)
    tables[:, 1, :, :, :, 0] ^= 1
    plan = jnp.asarray(tables.reshape(16, -1))[(2 * x + c) * 4 + z]
    out = jnp.full((genes_here, 2 * genes_here), grand * 0.0)
    scale = UNIT / cells_all
    held = {("own", 0): own_a, ("own", 1): own_b, (1, 0): d1a, (-1, 0): u1a, (1, 1): d1b, (-1, 1): u1b}
    products, narrow_products, received = [], [], []

    def work(slot, lefts, plan):
        product = products_of(plan, slot, lefts, [False, False, False, True], [held[n] for n in jobs[slot][0]])
        products.append(product)
        if slot < SLOTS - 1:
            narrow_products.append((product * scale).astype(jnp.float16))
            received.append(cross(narrow_products[-1], remote(slot)))

    plan, out = lax.optimization_barrier((plan, out))
    work(0, [own_a, own_b], plan)
    d2a, u2a = send(d1a, down(2)), send(u1a, up(2))
    d1b, u1b, _ = lax.optimization_barrier((d1b, u1b, narrow_products[0]))
    across, d1b, u1b, _ = lax.optimization_barrier((across, d1b, u1b, narrow_products[0]))
    held[1, 1], held[-1, 1], held[2, 0], held[-2, 0] = d1b, u1b, d2a, u2a
    d2b, u2b = send(d1b, down(2)), send(u1b, up(2))
    held[2, 1], held[-2, 1] = d2b, u2b
    lefts = [own_a, own_b, across, swap_core(across)]
    d3a, u3a = send(d2a, down(3)), send(u2a, up(3))
    work(1, lefts, after(plan, received[0], d2a, u2a))
    d2b, u2b, _ = lax.optimization_barrier((d2b, u2b, narrow_products[1]))
    d3b, u3b = send(d2b, down(3)), send(u2b, up(3))
    work(2, lefts, after(plan, narrow_products[1]))
    held[3, 0], held[-3, 0], held[3, 1], held[-3, 1] = d3a, u3a, d3b, u3b
    work(3, lefts, after(plan, narrow_products[2]))
    held["late", 0] = send(after(own_b, d3b, u3b), last)

    wide = lambda value: value.astype(jnp.float32)
    own_rows, other_rows = slice(0, genes_here), slice(genes_here, None)
    near_even, far_even = even & near_x, even & jnp.logical_not(near_x)
    near_end, far_end = odd_end & near_x, odd_end & jnp.logical_not(near_x)

    def total(mine, theirs, rows):
        return products[mine][rows] * scale + wide(received[theirs][rows])

    def mix(*choices):
        value = choices[-1]
        for condition, other in reversed(choices[:-1]):
            value = jnp.where(condition, other, value)
        return value

    def swap_some(value, devices):
        value = value.astype(jnp.float16)
        return value, swap_y(value, devices)

    def is_far_end(x, c, z):
        return is_odd_end(c, z) and not is_near(x, z)

    def is_far_even(x, c, z):
        return is_even(c, z) and not is_near(x, z)

    sent_a, got_a = swap_some(
        mix(
            (near_even, total(1, 1, own_rows)),
            (near_end, total(1, 1, other_rows)),
            total(3, 1, other_rows),
        ),
        lambda x, c, z: not is_far_end(x, c, z) and not is_far_even(x, c, z),
    )
    work(4, lefts, after(plan, narrow_products[3], sent_a))
    sent_b, got_b = swap_some(
        mix(
            (near_even, total(1, 1, other_rows)),
            (far_even, total(3, 2, other_rows)),
            total(4, 2, other_rows),
        ),
        lambda x, c, z: not is_odd_end(c, z),
    )
    plan = after(plan, narrow_products[4], sent_b)
    rights = [held[name] for name in jobs[5][0]]
    turned = [False, False, False, True]
    last_other = products_of(plan, 5, lefts, turned, rights, 2, 2)
    last_own = products_of(after(plan, last_other), 5, lefts, turned, rights, 0, 2)
    received[3] = after(received[3], last_own)
    _, got_c = swap_some(
        total(4, 3, other_rows), lambda x, c, z: is_far_end(x, c, z) or is_far_even(x, c, z)
    )

    def last_total(product, rows):
        return product * scale + wide(jnp.where(near_x, received[2][rows], received[4][rows]))

    _, got_d = swap_some(last_total(last_other, other_rows), lambda x, c, z: is_odd_end(c, z))

    own_first = mix(
        (near_even, total(0, 0, own_rows)),
        (far_even, total(3, 2, own_rows)),
        (near_end, total(1, 1, own_rows)),
        (far_end, total(4, 3, own_rows)),
        total(3, 1, own_rows),
    )
    own_second = mix(
        (near_even, total(0, 0, other_rows)),
        (far_even, total(4, 3, own_rows)),
        (odd_end, last_total(last_own, own_rows)),
        total(4, 2, own_rows),
    )
    got_first = wide(mix((far_even, got_b), (far_end, got_c), got_a))
    got_second = wide(mix((far_even, got_c), (odd_end, got_d), got_b))
    begin, begin_other = y * genes_here, (1 - y) * genes_here
    for value, place in (
        (own_first, begin + c * half),
        (got_first, begin_other + c * half),
        (own_second, begin + (1 - c) * half),
        (got_second, begin_other + (1 - c) * half),
    ):
        out = lax.dynamic_update_slice(out, value * (1.0 / UNIT), (0, place))
    return out


def body_any(counts):
    cells_all = counts.shape[0] * lax.axis_size("cell")
    values = counts.astype(jnp.float32)
    row_part = jnp.sum(values, axis=1)
    column_part = jnp.sum(values, axis=0)
    depths = lax.psum(row_part, "gene")
    gene_totals, grand_total = lax.psum((column_part, jnp.sum(depths)), "cell")
    expected = depths[:, None] * gene_totals[None, :] / grand_total
    scaled = (values - expected) / jnp.sqrt(expected + expected * expected / 100.0)
    ceiling = jnp.sqrt(jnp.float32(cells_all))
    residuals = jnp.clip(scaled, -ceiling, ceiling).astype(jnp.bfloat16)
    gathered = lax.all_gather(residuals, "gene", axis=1, tiled=True)
    owned_block = lax.psum_scatter(
        lax.dot_general(
            gathered, residuals, (((0,), (0,)), ((), ())), preferred_element_type=jnp.float32
        ),
        "cell",
        scatter_dimension=0,
        tiled=True,
    ).T
    return owned_block / jnp.float32(cells_all)


def solution(mesh):
    fits = (mesh.shape["cell"], mesh.shape["gene"]) == (4, 8)
    return jax.shard_map(
        body if fits else body_any,
        mesh=mesh,
        in_specs=(P("cell", "gene"),),
        out_specs=P("gene", "cell"),
        check_vma=False,
    )
```

```python
import math

import jax
import jax.numpy as jnp
import numpy as np
from jax import lax
from jax.experimental import pallas as pl
from jax.experimental.pallas import tpu as pltpu
from jax.sharding import PartitionSpec as P

AXES = ("cell", "gene")
UNIT = 8.0


def pairs_of(move):
    pairs = []
    for x in range(2):
        for c in range(2):
            for z in range(4):
                for y in range(2):
                    target = move(x, c, z, y)
                    if target is not None and 0 <= target[2] < 4:
                        tx, tc, tz, ty = target
                        pairs.append(((2 * x + c) * 8 + 2 * z + y, (2 * tx + tc) * 8 + 2 * tz + ty))
    return pairs


def send(value, move):
    return lax.ppermute(value, AXES, pairs_of(move))


def after(value, *others):
    return lax.optimization_barrier((value,) + others)[0]


VMEM = 48 * 2**20
SLOTS = 6
LIGHT = pl.CostEstimate(flops=0, bytes_accessed=0, transcendentals=0)


def residuals_of(near, far, depths, shares, part, parts, ceiling):
    cells, genes = near.shape
    width = genes // parts
    block = 512
    steps = cells // block
    lanes, group = 128, 32

    def kernel(part_ref, depth_ref, share_ref, near_ref, far_ref, out_ref):
        i = pl.program_id(0)
        depth = jnp.transpose(jnp.broadcast_to(depth_ref[...], (lanes, block)))

        def write(counts_ref):
            for r in range(0, block, group):
                for k in range(0, width, lanes):
                    expected = depth[r : r + group] * share_ref[:, k : k + lanes]
                    scale = lax.rsqrt(expected + expected * expected * 0.01)
                    values = counts_ref[r : r + group, k : k + lanes].astype(jnp.float32)
                    scaled = jnp.clip((values - expected) * scale, -ceiling, ceiling)
                    out_ref[r : r + group, k : k + lanes] = scaled.astype(jnp.bfloat16)

        @pl.when(i < steps)
        def _():
            write(near_ref)

        @pl.when(i >= steps)
        def _():
            write(far_ref)

    return pl.pallas_call(
        kernel,
        grid_spec=pltpu.PrefetchScalarGridSpec(
            num_scalar_prefetch=1,
            grid=(2 * steps,),
            in_specs=[
                pl.BlockSpec((1, block), lambda i, s: (0, i)),
                pl.BlockSpec((1, width), lambda i, s: (0, s[0])),
                pl.BlockSpec((block, width), lambda i, s: (jnp.minimum(i, steps - 1), s[0])),
                pl.BlockSpec((block, width), lambda i, s: (jnp.maximum(i - steps, 0), s[0])),
            ],
            out_specs=pl.BlockSpec((block, width), lambda i, s: (i, 0)),
        ),
        out_shape=jax.ShapeDtypeStruct((2 * cells, width), jnp.bfloat16),
        compiler_params=pltpu.CompilerParams(vmem_limit_bytes=VMEM),
        cost_estimate=pl.CostEstimate(
            flops=20 * cells * width, bytes_accessed=12 * cells * width, transcendentals=2 * cells * width
        ),
    )(jnp.reshape(part, (1,)).astype(jnp.int32), depths.reshape(1, -1), shares.reshape(1, -1), near, far)


def products_of(plan, slot, lefts, turned, rights, first=0, blocks=4):
    rows, width = rights[0].shape
    upper = rows // 2
    base = (slot * 4 + first) * 2
    n_left = len(lefts)

    def kernel(s, *refs):
        left_refs, right_refs = refs[:n_left], refs[n_left : n_left + len(rights)]
        out_ref, left_buf, right_buf, left_sem, right_sem = refs[n_left + len(rights) :]
        i = pl.program_id(0)

        def left_at(block):
            return s[base + 2 * block]

        def right_at(block):
            return s[base + 2 * block + 1]

        def left_copies(n, to):
            for part in range(2):
                place = 1 - part if turned[n] else part
                yield pltpu.make_async_copy(
                    left_refs[n].at[pl.ds(part * upper, upper)],
                    left_buf.at[to, pl.ds(place * upper, upper)],
                    left_sem.at[to, part],
                )

        def fetch(block, to):
            for n in range(n_left):
                @pl.when(left_at(block) == n)
                def _(n=n):
                    for copy in left_copies(n, to):
                        copy.start()

        def arrive(block, to):
            for n in range(n_left):
                @pl.when(left_at(block) == n)
                def _(n=n):
                    for copy in left_copies(n, to):
                        copy.wait()

        @pl.when(i == 0)
        def _():
            fetch(0, 0)
            fetch(1, 1)

        @pl.when((i == 0) | (right_at(i) != right_at(jnp.maximum(i - 1, 0))))
        def _():
            for n, ref in enumerate(right_refs):
                @pl.when(right_at(i) == n)
                def _(ref=ref):
                    copy = pltpu.make_async_copy(ref, right_buf, right_sem)
                    copy.start()
                    copy.wait()

        for to in range(2):
            @pl.when(lax.rem(i, 2) == to)
            def _(to=to):
                arrive(i, to)

                @pl.when((i > 0) & (i + 1 < blocks))
                def _():
                    fetch(i + 1, 1 - to)

                out_ref[...] = lax.dot_general(
                    left_buf[to], right_buf[...], (((0,), (0,)), ((), ())), preferred_element_type=jnp.float32
                )

    return pl.pallas_call(
        kernel,
        grid_spec=pltpu.PrefetchScalarGridSpec(
            num_scalar_prefetch=1,
            grid=(blocks,),
            in_specs=[pl.BlockSpec(memory_space=pl.ANY)] * (n_left + len(rights)),
            out_specs=pl.BlockSpec((width, width), lambda i, s: (i, 0)),
            scratch_shapes=[
                pltpu.VMEM((2, rows, width), jnp.bfloat16),
                pltpu.VMEM((rows, width), jnp.bfloat16),
                pltpu.SemaphoreType.DMA((2, 2)),
                pltpu.SemaphoreType.DMA,
            ],
        ),
        out_shape=jax.ShapeDtypeStruct((blocks * width, width), jnp.float32),
        compiler_params=pltpu.CompilerParams(vmem_limit_bytes=VMEM),
        cost_estimate=pl.CostEstimate(
            flops=8 * rows * blocks * width * width,
            bytes_accessed=2 * (blocks + 1) * rows * width + 4 * blocks * width * width,
            transcendentals=0,
        ),
    )(plan, *lefts, *rights)


def is_even(c, z):
    return c == z % 2


def is_near(x, z):
    return x == z // 2


def is_end(z):
    return z in (0, 3)


def job(x, c, z, slot):
    near, first = is_near(x, z), 1 if z == 0 or (z != 3 and x == 0) else -1
    far = 2 if z < 2 else -2
    if is_even(c, z):
        if slot == 0:
            return "own rows", not near
        if not near:
            return [None, ("other rows", True), None, ((far, 0), False), ((far, 1), False), None][slot]
        return [None, ("other rows", False), ((far, 0), True), ((far, 1), True), None, None][slot]
    if not is_end(z):
        return [None, ((first, 0), True), ((first, 1), True), ((-first, 0), False), ((-first, 1), False), None][slot]
    far = 3 if z == 0 else -3
    if near:
        return [None, ((first, 0), False), None, ((far, 0), True), ((far, 1), True), ((first, 1), False)][slot]
    return [None, ((first, 0), True), ((first, 1), True), None, ((far, 0), False), ((far, 1), False)][slot]


def remote(slot):
    def devices(x, c, z):
        work = job(x, c, z, slot)
        return work is not None and work[1]
    return devices


def rights_of(slot):
    names, table = [("own", 0), ("own", 1)] if slot < 2 else [], np.zeros((2, 2, 4, 4, 2), np.int32)
    for x in range(2):
        for c in range(2):
            for z in range(4):
                work = job(x, c, z, slot)
                if work is None:
                    continue
                if work[0] in ("own rows", "other rows"):
                    rows = (0, 1) if work[0] == "own rows" else (2, 3)
                    pairs = [(row, ("own", half)) for half in range(2) for row in rows]
                else:
                    name = ("late", 0) if slot == 5 and abs(work[0][0]) == 1 else work[0]
                    pairs = [(row, name) for row in range(4)]
                for i, (row, name) in enumerate(pairs):
                    if name not in names:
                        names.append(name)
                    table[x, c, z, i] = row, names.index(name)
    return names, table


def body(counts):
    cells_here, genes_here = counts.shape
    cells_all = cells_here * lax.axis_size("cell")
    half = genes_here // 2
    cell, gene = lax.axis_index("cell"), lax.axis_index("gene")
    x, c, z, y = cell // 2, cell % 2, gene // 2, gene % 2
    even = c == z % 2
    low = z < 2
    end = (z == 0) | (z == 3)
    odd_end = end & jnp.logical_not(even)
    near_x = (x == 0) == low

    def is_odd_end(c, z):
        return not is_even(c, z) and is_end(z)

    def down(distance):
        def move(x, c, z, y):
            source = z + distance - 1
            if c != source % 2 or source > 3 or (distance == 1 and x == 0 and z == 1):
                return None
            return x, c, z - 1, y
        return move

    def up(distance):
        def move(x, c, z, y):
            source = z - distance + 1
            if c != source % 2 or source < 0 or (distance == 1 and x == 1 and z == 2):
                return None
            return x, c, z + 1, y
        return move

    def last(x, c, z, y):
        if x == 0 and c == 1 and z == 1:
            return x, c, 0, y
        if x == 1 and c == 0 and z == 2:
            return x, c, 3, y
        return None

    def down_all(x, c, z, y):
        return (x, c, z - 1, y) if c == z % 2 else None

    def up_all(x, c, z, y):
        return (x, c, z + 1, y) if c == z % 2 else None

    def swap_core(value):
        return send(value, lambda x, c, z, y: (x, 1 - c, z, y))

    def swap_y(value, devices=lambda x, c, z: True):
        return send(value, lambda x, c, z, y: (x, c, z, 1 - y) if devices(x, c, z) else None)

    def cross(value, devices):
        return send(value, lambda x, c, z, y: (1 - x, c, z, y) if devices(x, c, z) else None)

    sibling = swap_core(counts)
    row_part = jnp.sum(counts, axis=1)
    totals = jnp.sum(counts, axis=0)
    both = swap_core(jnp.concatenate([totals, row_part]))
    beside = [
        send(totals, lambda x, c, z, y: (1 - x, c, z, y)),
        send(totals, lambda x, c, z, y: (1 - x, 1 - c, z, y)),
    ]
    totals = totals + both[:genes_here] + beside[0] + beside[1]
    row_part = jnp.concatenate([row_part, both[genes_here:]])
    got = swap_y(jnp.concatenate([totals, row_part]))
    message = jnp.concatenate([totals, got[:genes_here], row_part + got[genes_here:]])
    messages = jnp.stack(
        [message]
        + [send(message, lambda x, c, z, y, bits=bits: (x, c, z ^ bits, y)) for bits in (1, 2, 3)]
    )
    depths = jnp.sum(messages[:, 2 * genes_here :], axis=0).astype(jnp.float32)
    grand = jnp.sum(messages[:, : 2 * genes_here].astype(jnp.float32))
    ceiling = math.sqrt(cells_all)
    shares = totals.astype(jnp.float32) / grand

    own_a = residuals_of(counts, sibling, depths, shares, c, 2, ceiling)
    d1a, u1a = send(own_a, down_all), send(own_a, up_all)
    own_b = residuals_of(counts, sibling, depths, shares, 1 - c, 2, ceiling)
    d1b, u1b = send(own_b, down(1)), send(own_b, up(1))
    across = swap_y(after(own_a, own_b))

    jobs = [rights_of(slot) for slot in range(SLOTS)]
    tables = np.stack([table for _, table in jobs], axis=3)
    tables[:, 1, :, :, :, 0] ^= 1
    plan = jnp.asarray(tables.reshape(16, -1))[(2 * x + c) * 4 + z]
    out = jnp.full((genes_here, 2 * genes_here), grand * 0.0)
    scale = UNIT / cells_all
    held = {("own", 0): own_a, ("own", 1): own_b, (1, 0): d1a, (-1, 0): u1a, (1, 1): d1b, (-1, 1): u1b}
    products, narrow_products, received = [], [], []

    def work(slot, lefts, plan):
        product = products_of(plan, slot, lefts, [False, False, False, True], [held[n] for n in jobs[slot][0]])
        products.append(product)
        if slot < SLOTS - 1:
            narrow_products.append((product * scale).astype(jnp.float16))
            received.append(cross(narrow_products[-1], remote(slot)))

    plan, out = lax.optimization_barrier((plan, out))
    work(0, [own_a, own_b], plan)
    d2a, u2a = send(d1a, down(2)), send(u1a, up(2))
    d1b, u1b, _ = lax.optimization_barrier((d1b, u1b, narrow_products[0]))
    across, d1b, u1b, _ = lax.optimization_barrier((across, d1b, u1b, narrow_products[0]))
    held[1, 1], held[-1, 1], held[2, 0], held[-2, 0] = d1b, u1b, d2a, u2a
    d2b, u2b = send(d1b, down(2)), send(u1b, up(2))
    held[2, 1], held[-2, 1] = d2b, u2b
    lefts = [own_a, own_b, across, swap_core(across)]
    d3a, u3a = send(d2a, down(3)), send(u2a, up(3))
    work(1, lefts, after(plan, received[0], d2a, u2a))
    d2b, u2b, _ = lax.optimization_barrier((d2b, u2b, narrow_products[1]))
    d3b, u3b = send(d2b, down(3)), send(u2b, up(3))
    work(2, lefts, after(plan, narrow_products[1]))
    held[3, 0], held[-3, 0], held[3, 1], held[-3, 1] = d3a, u3a, d3b, u3b
    work(3, lefts, after(plan, narrow_products[2]))
    held["late", 0] = send(after(own_b, d3b, u3b), last)

    wide = lambda value: value.astype(jnp.float32)
    own_rows, other_rows = slice(0, genes_here), slice(genes_here, None)
    near_even, far_even = even & near_x, even & jnp.logical_not(near_x)
    near_end, far_end = odd_end & near_x, odd_end & jnp.logical_not(near_x)

    def total(mine, theirs, rows):
        return products[mine][rows] * scale + wide(received[theirs][rows])

    def mix(*choices):
        value = choices[-1]
        for condition, other in reversed(choices[:-1]):
            value = jnp.where(condition, other, value)
        return value

    def swap_some(value, devices):
        value = value.astype(jnp.float16)
        return value, swap_y(value, devices)

    def is_far_end(x, c, z):
        return is_odd_end(c, z) and not is_near(x, z)

    def is_far_even(x, c, z):
        return is_even(c, z) and not is_near(x, z)

    sent_a, got_a = swap_some(
        mix(
            (near_even, total(1, 1, own_rows)),
            (near_end, total(1, 1, other_rows)),
            total(3, 1, other_rows),
        ),
        lambda x, c, z: not is_far_end(x, c, z) and not is_far_even(x, c, z),
    )
    work(4, lefts, after(plan, narrow_products[3], sent_a))
    sent_b, got_b = swap_some(
        mix(
            (near_even, total(1, 1, other_rows)),
            (far_even, total(3, 2, other_rows)),
            total(4, 2, other_rows),
        ),
        lambda x, c, z: not is_odd_end(c, z),
    )
    plan = after(plan, narrow_products[4], sent_b)
    rights = [held[name] for name in jobs[5][0]]
    turned = [False, False, False, True]
    last_other = products_of(plan, 5, lefts, turned, rights, 2, 2)
    last_own = products_of(after(plan, last_other), 5, lefts, turned, rights, 0, 2)
    received[3] = after(received[3], last_own)
    _, got_c = swap_some(
        total(4, 3, other_rows), lambda x, c, z: is_far_end(x, c, z) or is_far_even(x, c, z)
    )

    def last_total(product, rows):
        return product * scale + wide(jnp.where(near_x, received[2][rows], received[4][rows]))

    _, got_d = swap_some(last_total(last_other, other_rows), lambda x, c, z: is_odd_end(c, z))

    own_first = mix(
        (near_even, total(0, 0, own_rows)),
        (far_even, total(3, 2, own_rows)),
        (near_end, total(1, 1, own_rows)),
        (far_end, total(4, 3, own_rows)),
        total(3, 1, own_rows),
    )
    own_second = mix(
        (near_even, total(0, 0, other_rows)),
        (far_even, total(4, 3, own_rows)),
        (odd_end, last_total(last_own, own_rows)),
        total(4, 2, own_rows),
    )
    got_first = wide(mix((far_even, got_b), (far_end, got_c), got_a))
    got_second = wide(mix((far_even, got_c), (odd_end, got_d), got_b))
    begin, begin_other = y * genes_here, (1 - y) * genes_here
    for value, place in (
        (own_first, begin + c * half),
        (got_first, begin_other + c * half),
        (own_second, begin + (1 - c) * half),
        (got_second, begin_other + (1 - c) * half),
    ):
        out = lax.dynamic_update_slice(out, value * (1.0 / UNIT), (0, place))
    return out


def body_any(counts):
    cells_all = counts.shape[0] * lax.axis_size("cell")
    values = counts.astype(jnp.float32)
    row_part = jnp.sum(values, axis=1)
    column_part = jnp.sum(values, axis=0)
    depths = lax.psum(row_part, "gene")
    gene_totals, grand_total = lax.psum((column_part, jnp.sum(depths)), "cell")
    expected = depths[:, None] * gene_totals[None, :] / grand_total
    scaled = (values - expected) / jnp.sqrt(expected + expected * expected / 100.0)
    ceiling = jnp.sqrt(jnp.float32(cells_all))
    residuals = jnp.clip(scaled, -ceiling, ceiling).astype(jnp.bfloat16)
    gathered = lax.all_gather(residuals, "gene", axis=1, tiled=True)
    owned_block = lax.psum_scatter(
        lax.dot_general(
            gathered, residuals, (((0,), (0,)), ((), ())), preferred_element_type=jnp.float32
        ),
        "cell",
        scatter_dimension=0,
        tiled=True,
    ).T
    return owned_block / jnp.float32(cells_all)


def solution(mesh):
    fits = (mesh.shape["cell"], mesh.shape["gene"]) == (4, 8)
    return jax.shard_map(
        body if fits else body_any,
        mesh=mesh,
        in_specs=(P("cell", "gene"),),
        out_specs=P("gene", "cell"),
        check_vma=False,
    )
```
